512 devices in a mesh: language: 8 (over y_hi, core), fsdp: 64 (over y_lo, x, z).
Axes of the slice: x: 4, y: 8 (y_hi: 4, y_lo: 2; y = y_hi * 2 + y_lo), z: 8, core: 2. Of those that a mesh axis runs over, the one named last changes fastest.
Arguments:
- hidden: bfloat16 [16, 8192, 5120], P('language', 'fsdp'), may hold values from -60 to 60
- latent_grad: bfloat16 [16, 8192, 64], P('language', 'fsdp'), may hold values from -0.15625 to 0.15625
- lang_ids: int32 [16], P('language'), may hold values from 0 to 15, each once
- old_weights: float32 [16], replicated, may hold values from 0.02 to 0.2
- param: float32 [5120, 64], P('fsdp'), may hold values from -6 to 6
- first_moment: float32 [5120, 64], P('fsdp'), may hold values from -6 to 6
- second_moment: float32 [5120, 64], P('fsdp'), may hold values from 0.25 to 4
Outputs:
- new_param: float32 [5120, 64], P('fsdp')
- new_first: float32 [5120, 64], P('fsdp')
- new_second: float32 [5120, 64], P('fsdp')
- new_logweights: float32 [16], replicated
The draws below stay inside these ranges and needn't reach their ends.
Inputs may be any that keep to these rules, and one draw needn't show every extreme that they name: `lang_ids`: each id appears in exactly one slot.
All inputs are finite; a program needn't handle non-finite values.
Results may differ from the reference program's by a relative error of at most 0.0003.
Values may be sent and summed in bfloat16 or wider, within the bound.
A program may use at most 64 MiB of HBM per device.

```python
import math
import jax
import jax.numpy as jnp
from jax import lax

D = 5120
RANK = 32
STEP = 100
LANGS = 16
TOKENS = 8192


def draw_hidden(key, part):
    key_lang, key_feat, key_base = jax.random.split(key, 3)
    lang_scale = jnp.exp(jax.random.uniform(key_lang, (LANGS, 1, 1), minval=math.log(0.5), maxval=math.log(2.0)))
    position = jnp.arange(D, dtype=jnp.float32) / D
    feat_scale = jnp.exp(0.55 * position + 0.3 * jax.random.normal(key_feat, (D,), dtype=jnp.float32))
    base = jax.random.normal(key_base, (LANGS, TOKENS, D), dtype=jnp.float32)
    values = jnp.clip(base * lang_scale * feat_scale[None, None, :], -60.0, 60.0)
    return values.astype(jnp.bfloat16)


def block_levels(own_key, dims, shards, smallest, top_value):
    def one(axis_at, parts):
        heights = jax.random.uniform(jax.random.fold_in(jax.random.fold_in(own_key, 6), axis_at), (parts,), jnp.float32, smallest / len(shards), top_value / len(shards))
        return jnp.repeat(jnp.exp(heights), dims[axis_at] // parts).reshape((-1,) + (1,) * (len(dims) - axis_at - 1))

    loudness = one(*shards[0])
    for cut in shards[1:]:
        loudness = loudness * one(*cut)
    return loudness


def normal_values(key, shape, deviation, most, shards=(), kind=jnp.bfloat16):
    array = jax.random.normal(key, shape, jnp.float32) * deviation
    if len(shards) > 0:
        array = block_levels(key, shape, shards, -0.22, 0.18) * array
    return jnp.clip(array, min=-most, max=most).astype(kind)


def setup_inputs(seed: int = 0) -> dict:
    streams_of = jax.random.split(jax.random.key(seed), 8)
    hidden = draw_hidden(jax.random.fold_in(streams_of[7], 71), 0)
    latent_grad = normal_values(streams_of[1], (LANGS, TOKENS, 2 * RANK), (1.0 / TOKENS ** 0.5), 0.15625, ((0, 8), (1, 64)))
    lang_ids = jax.random.permutation(streams_of[2], LANGS).astype(jnp.int32)
    old_weights = jnp.clip(jnp.exp(jax.random.uniform(streams_of[3], (LANGS,), jnp.float32, math.log(0.02), math.log(0.2))), 0.02, 0.2)
    param = normal_values(streams_of[4], (D, 2 * RANK), 1.0, 6.0, ((0, 64),), jnp.float32)
    first_moment = normal_values(streams_of[5], (D, 2 * RANK), 1.0, 6.0, ((0, 64),), jnp.float32)
    second_moment = jnp.clip(jnp.exp(math.log(4.0) - 2.7725887 * jax.random.uniform(streams_of[6], (D, 2 * RANK), jnp.float32) ** block_levels(streams_of[6], (D, 2 * RANK), ((0, 64),), -0.2, 0.2)), 0.25, 4.0)
    return {"hidden": hidden, "latent_grad": latent_grad, "lang_ids": lang_ids, "old_weights": old_weights, "param": param, "first_moment": first_moment, "second_moment": second_moment}


def slot_gradient(pair):
    feats, latents = pair
    return jnp.einsum('td,tr->dr', feats.astype(jnp.float32), latents.astype(jnp.float32), precision=lax.Precision.HIGHEST)

def reference(hidden, latent_grad, lang_ids, old_weights, param, first_moment, second_moment):
    slot_grad = lax.map(slot_gradient, (hidden, latent_grad))
    total = lax.optimization_barrier(jnp.sum(slot_grad, axis=0))
    dots = jnp.einsum('ldr,dr->l', slot_grad, total, precision=lax.Precision.HIGHEST)
    square = jnp.sum(total * total) + 1e-06
    onehot = (lang_ids[:, None] == jnp.arange(LANGS, dtype=jnp.int32)[None, :]).astype(jnp.float32)
    align = jnp.dot(dots, onehot, precision=lax.Precision.HIGHEST) / square
    logits = jnp.log(old_weights) + LANGS * align
    new_logweights = logits - jnp.log(jnp.sum(jnp.exp(logits)))
    weights = jnp.exp(new_logweights)
    slot_weight = jnp.dot(onehot, weights, precision=lax.Precision.HIGHEST)
    update = jnp.einsum('l,ldr->dr', slot_weight, slot_grad, precision=lax.Precision.HIGHEST)
    new_first = 0.9 * first_moment + 0.1 * update
    new_second = 0.95 * second_moment + 0.05 * update * update
    first_hat = new_first / (1.0 - 0.9 ** STEP)
    second_hat = new_second / (1.0 - 0.95 ** STEP)
    new_param = param - 0.02 * (first_hat / (jnp.sqrt(second_hat) + 1e-08) + 0.1 * param)
    return (new_param, new_first, new_second, new_logweights)
```

```python
import functools

import jax
import jax.numpy as jnp
from jax import lax
from jax.experimental import pallas as pl
from jax.experimental.pallas import tpu as pltpu
from jax.sharding import PartitionSpec as P

STEP = 100
GRID = {64: (2, 4, 8), 8: (2, 2, 2)}
RY, RX, RZ = 32, 32, 16
F32 = jnp.float32
WIRE = jnp.float32


def kernel(
    nl, ny, nx, nz,
    hid, lat, ids, old, param, first, second,
    new_param, new_first, new_second, new_logw,
    hv, ys, xs, zs, yr, xr, zr, y2s, x2s, z2s, y2r, x2r, z2r, y3s, x3s, z3s, y3r, x3r, z3r,
    gath, oh, ar1, ar2,
    hsem, ysend, yrecv, xsend, xrecv, zsend, zrecv,
    y2send, y2recv, x2send, x2recv, z2send, z2recv,
    y3send, y3recv, x3send, x3recv, z3send, z3recv,
    gsend, grecv, osend, orecv, a1send, a1recv, a2send, a2recv,
):
    g = lax.axis_index("language")
    f = lax.axis_index("fsdp")
    y = f // (nx * nz)
    x = (f // nz) % nx
    z = f % nz
    ranks = lat.shape[1]
    toks = hid.shape[1]
    cols = 2 * ranks
    blk = hid.shape[2] // (ny * nx)

    def at(yy, xx, zz):
        return {"fsdp": (yy * nx + xx) * nz + zz, "language": g}

    def lang(gg):
        return {"fsdp": f, "language": gg}

    def hop(v, d, n):
        return lax.rem(v + d, n)

    zpeers = [at(y, x, hop(z, d, nz)) for d in range(1, nz)]
    xpeers = [at(y, hop(x, d, nx), z) for d in range(1, nx)]
    ypeer = at(1 - y, x, z)
    diag = [at(1 - y, hop(x, d, nx), z) for d in range(1, nx)]
    lpeers = [lang(hop(g, d, nl)) for d in range(1, nl)]
    peers = [ypeer] + xpeers + zpeers + lpeers + diag

    barrier = pltpu.get_barrier_semaphore()
    for p in peers:
        pl.semaphore_signal(barrier, inc=1, device_id=p, device_id_type=pl.DeviceIdType.MESH)

    def send(src, dst, ssem, rsem, dev):
        c = pltpu.make_async_remote_copy(
            src_ref=src, dst_ref=dst, send_sem=ssem, recv_sem=rsem,
            device_id=dev, device_id_type=pl.DeviceIdType.MESH,
        )
        c.start()
        sent.append(c)

    def wait(dst, rsem):
        pltpu.make_async_copy(dst, dst, rsem).wait()

    sent = []
    xorder = [2, 1, 3, 0] if nx == 4 else list(range(1, nx)) + [0]
    order = [(dy, dx) for dy in (1, 0) for dx in xorder]
    loads = []
    for i, (dy, dx) in enumerate(order):
        c = hop(y, dy, ny) * nx + hop(x, dx, nx)
        at0 = c * blk
        if blk % 128 == 0:
            at0 = pl.multiple_of(at0, 128)
        cp = pltpu.make_async_copy(hid.at[:, :, pl.ds(at0, blk)], hv.at[i], hsem.at[i])
        cp.start()
        loads.append(cp)

    lane = lax.broadcasted_iota(jnp.int32, (1, 128), 1)
    row = lax.broadcasted_iota(jnp.int32, (2, 128), 0)
    lane2 = lax.broadcasted_iota(jnp.int32, (2, 128), 1)
    mine = jnp.where(row == 0, ids[0], ids[1])
    oh[g] = (mine == lane2).astype(F32)
    weights_old = jnp.ones((1, 128), F32)
    for k in range(old.shape[0]):
        weights_old = jnp.where(lane == k, old[k], weights_old)

    zero = jnp.zeros((ranks, toks), jnp.bfloat16)
    lhs = jnp.concatenate(
        [jnp.concatenate([lat[0], zero], axis=1), jnp.concatenate([zero, lat[1]], axis=1)], axis=0
    )

    for i, (dy, dx) in enumerate(order):
        yy, xx = hop(y, dy, ny), hop(x, dx, nx)
        loads[i].wait()
        rhs = hv[i].reshape(2 * toks, blk)
        part = jnp.dot(lhs, rhs, preferred_element_type=F32)
        part = part.T.reshape(nz, RY + RX + RZ, cols).astype(WIRE)
        ys[yy, xx] = part[:, :RY]
        xs[xx, yy] = part[:, RY : RY + RX]
        zs[:, yy, xx] = part[:, RY + RX :]
        if i == 0:
            pl.semaphore_wait(barrier, len(peers))
        if dy:
            send(ys.at[yy, xx], yr.at[xx], ysend.at[dx], yrecv.at[dx], ypeer)
        if dx:
            send(xs.at[xx, yy], xr.at[dx - 1, yy], xsend.at[dx - 1, dy], xrecv.at[dx - 1, dy], xpeers[dx - 1])
    for d in range(1, nz):
        send(zs.at[hop(z, d, nz)], zr.at[d - 1], zsend.at[d - 1], zrecv.at[d - 1], zpeers[d - 1])
    for d in range(1, nl):
        send(oh.at[g], oh.at[g], osend.at[d - 1], orecv.at[d - 1], lpeers[d - 1])

    for dx in xorder:
        xx = hop(x, dx, nx)
        wait(yr.at[xx], yrecv.at[dx])
        y2s[xx] = (ys[y, xx].astype(F32) + yr[xx].astype(F32)).astype(WIRE)
        if dx:
            send(y2s.at[xx], y2r.at[dx - 1], y2send.at[dx - 1], y2recv.at[dx - 1], xpeers[dx - 1])
    for dy in (1, 0):
        yy = hop(y, dy, ny)
        acc = xs[x, yy].astype(F32)
        for d in range(1, nx):
            wait(xr.at[d - 1, yy], xrecv.at[d - 1, dy])
            acc = acc + xr[d - 1, yy].astype(F32)
        x2s[yy] = acc.astype(WIRE)
        if dy:
            send(x2s.at[yy], x2r, x2send, x2recv, ypeer)
    acc = zs[z].astype(F32)
    for d in range(1, nz):
        wait(zr.at[d - 1], zrecv.at[d - 1])
        acc = acc + zr[d - 1].astype(F32)
    z2s[...] = acc.astype(WIRE)
    send(z2s.at[1 - y], z2r, z2send, z2recv, ypeer)

    wait(x2r, x2recv)
    x3s[...] = (x2s[y].astype(F32) + x2r[...].astype(F32)).astype(WIRE)
    for d in range(1, nz):
        send(x3s.at[hop(z, d, nz)], x3r.at[d - 1], x3send.at[d - 1], x3recv.at[d - 1], zpeers[d - 1])
    acc = y2s[x].astype(F32)
    for d in range(1, nx):
        wait(y2r.at[d - 1], y2recv.at[d - 1])
        acc = acc + y2r[d - 1].astype(F32)
    y3s[...] = acc.astype(WIRE)
    for d in range(1, nz):
        send(y3s.at[hop(z, d, nz)], y3r.at[d - 1], y3send.at[d - 1], y3recv.at[d - 1], zpeers[d - 1])
    wait(z2r, z2recv)
    z3s[...] = (z2s[y].astype(F32) + z2r[...].astype(F32)).astype(WIRE)
    for d in range(1, nx):
        send(z3s.at[hop(x, d, nx)], z3r.at[d - 1], z3send.at[d - 1], z3recv.at[d - 1], xpeers[d - 1])

    parts = ((0, RY), (RY, RX), (RY + RX, RZ))

    def finish(own, r, rsem, n, part):
        lo, size = parts[part]
        acc = own.astype(F32)
        for d in range(1, n):
            wait(r.at[d - 1], rsem.at[d - 1])
            acc = acc + r[d - 1].astype(F32)
        gath[g, lo : lo + size] = acc.astype(WIRE)
        for d in range(1, nl):
            ref = gath.at[g, pl.ds(lo, size)]
            send(ref, ref, gsend.at[part, d - 1], grecv.at[part, d - 1], lpeers[d - 1])

    finish(x3s[z], x3r, x3recv, nz, 1)
    finish(z3s[x], z3r, z3recv, nx, 2)
    finish(y3s[z], y3r, y3recv, nz, 0)

    for d in range(1, nl):
        src = hop(g, nl - d, nl)
        wait(oh.at[src], orecv.at[d - 1])
        for part, (lo, size) in enumerate(parts):
            wait(gath.at[src, pl.ds(lo, size)], grecv.at[part, d - 1])

    slots = gath[...].astype(F32)
    total = jnp.sum(slots, axis=0)
    both = total + pltpu.roll(total, ranks, 1)
    prods = jnp.sum(slots * both[None], axis=1)
    first_slot = lane < ranks
    dot0 = jnp.sum(jnp.where(first_slot, prods, 0.0), axis=1, keepdims=True)
    dot1 = jnp.sum(jnp.where(first_slot, 0.0, prods), axis=1, keepdims=True)
    square = jnp.sum(jnp.where(first_slot, jnp.sum(both * both, axis=0, keepdims=True), 0.0), axis=1, keepdims=True)
    oh0, oh1 = oh[:, 0, :], oh[:, 1, :]
    vec = jnp.sum(oh0 * dot0 + oh1 * dot1, axis=0, keepdims=True)
    langs = old.shape[0]
    vec = jnp.where(lane == langs, square, vec)

    ar1[z] = vec
    for d in range(1, nz):
        send(ar1.at[z], ar1.at[z], a1send.at[d - 1], a1recv.at[d - 1], zpeers[d - 1])
    for d in range(1, nz):
        wait(ar1.at[hop(z, nz - d, nz)], a1recv.at[d - 1])
    vec = jnp.sum(ar1[...], axis=0)
    me = y * nx + x
    ar2[me] = vec
    for dy in range(ny):
        for dx in range(nx):
            j = dy * nx + dx
            if j:
                dev = xpeers[dx - 1] if dy == 0 else (diag[dx - 1] if dx else ypeer)
                send(ar2.at[me], ar2.at[me], a2send.at[j - 1], a2recv.at[j - 1], dev)
    for dy in range(ny):
        for dx in range(nx):
            j = dy * nx + dx
            if j:
                src = hop(y, ny - dy, ny) * nx + hop(x, nx - dx, nx)
                wait(ar2.at[src], a2recv.at[j - 1])
    vec = jnp.sum(ar2[...], axis=0)

    square = jnp.sum(jnp.where(lane == langs, vec, 0.0), axis=1, keepdims=True) + 1e-06
    valid = lane < langs
    logits = jnp.log(weights_old) + langs * (jnp.where(valid, vec, 0.0) / square)
    norm = jnp.log(jnp.sum(jnp.where(valid, jnp.exp(logits), 0.0), axis=1, keepdims=True))
    logw = logits - norm
    new_logw[...] = logw
    weights = jnp.where(valid, jnp.exp(logw), 0.0)
    w0 = jnp.sum(oh0 * weights, axis=1, keepdims=True)
    w1 = jnp.sum(oh1 * weights, axis=1, keepdims=True)
    slot_weight = jnp.where(first_slot, w0, w1)
    update = jnp.sum(slots * slot_weight[:, None, :], axis=0).T
    update = update[:ranks] + update[ranks:]
    m = 0.9 * first[...] + 0.1 * update
    v = 0.95 * second[...] + 0.05 * update * update
    new_first[...] = m
    new_second[...] = v
    m_hat = m / (1.0 - 0.9**STEP)
    v_hat = v / (1.0 - 0.95**STEP)
    p = param[...]
    new_param[...] = p - 0.02 * (m_hat / (jnp.sqrt(v_hat) + 1e-08) + 0.1 * p)

    for c in sent:
        c.wait_send()


def local(nl, ny, nx, nz, hidden, latent_grad, lang_ids, old_weights, param, first_moment, second_moment):
    rows, ranks = param.shape
    cols = 2 * ranks
    assert rows == RY + RX + RZ and hidden.shape[0] == 2
    blk = hidden.shape[2] // (ny * nx)
    vmem = pl.BlockSpec(memory_space=pltpu.VMEM)
    smem = pl.BlockSpec(memory_space=pltpu.SMEM)
    dma = pltpu.SemaphoreType.DMA
    b = lambda *s: pltpu.VMEM(s + (cols,), WIRE)
    mat = jax.ShapeDtypeStruct((ranks, rows), F32)
    scratch = [
        pltpu.VMEM((ny * nx, 2, hidden.shape[1], blk), jnp.bfloat16),
        b(ny, nx, nz, RY), b(nx, ny, nz, RX), b(nz, ny, nx, RZ),
        b(nx, nz, RY), b(nx - 1, ny, nz, RX), b(nz - 1, ny, nx, RZ),
        b(nx, nz, RY), b(ny, nz, RX), b(ny, nx, RZ),
        b(nx - 1, nz, RY), b(nz, RX), b(nx, RZ),
        b(nz, RY), b(nz, RX), b(nx, RZ),
        b(nz - 1, RY), b(nz - 1, RX), b(nx - 1, RZ),
        b(nl, rows),
        pltpu.VMEM((nl, 2, 128), F32),
        pltpu.VMEM((nz, 1, 128), F32),
        pltpu.VMEM((ny * nx, 1, 128), F32),
        dma((ny * nx,)),
        dma((nx,)), dma((nx,)), dma((nx - 1, ny)), dma((nx - 1, ny)), dma((nz - 1,)), dma((nz - 1,)),
        dma((nx - 1,)), dma((nx - 1,)), dma, dma, dma, dma,
        dma((nz - 1,)), dma((nz - 1,)), dma((nz - 1,)), dma((nz - 1,)), dma((nx - 1,)), dma((nx - 1,)),
        dma((3, nl - 1)), dma((3, nl - 1)), dma((nl - 1,)), dma((nl - 1,)),
        dma((nz - 1,)), dma((nz - 1,)), dma((ny * nx - 1,)), dma((ny * nx - 1,)),
    ]
    outs = pl.pallas_call(
        functools.partial(kernel, nl, ny, nx, nz),
        out_shape=(mat, mat, mat, jax.ShapeDtypeStruct((1, 128), F32)),
        in_specs=[pl.BlockSpec(memory_space=pl.ANY), vmem, smem, smem, vmem, vmem, vmem],
        out_specs=(vmem, vmem, vmem, vmem),
        scratch_shapes=scratch,
        compiler_params=pltpu.CompilerParams(
            collective_id=0, has_side_effects=True, vmem_limit_bytes=61 * 1024 * 1024
        ),
        name="reweighted_step",
    )(
        hidden, latent_grad.transpose(0, 2, 1), lang_ids, old_weights,
        param.T, first_moment.T, second_moment.T,
    )
    return (outs[0].T, outs[1].T, outs[2].T, outs[3][0, : old_weights.shape[0]])


def solution(mesh):
    nl = mesh.shape["language"]
    ny, nx, nz = GRID[mesh.shape["fsdp"]]
    placed = (
        P("language", "fsdp", None),
        P("language", "fsdp", None),
        P("language"),
        P(),
        P("fsdp", None),
        P("fsdp", None),
        P("fsdp", None),
    )
    return jax.shard_map(
        functools.partial(local, nl, ny, nx, nz),
        mesh=mesh,
        in_specs=placed,
        out_specs=(P("fsdp", None), P("fsdp", None), P("fsdp", None), P()),
        check_vma=False,
    )
```

```python
import functools

import jax
import jax.numpy as jnp
from jax import lax
from jax.experimental import pallas as pl
from jax.experimental.pallas import tpu as pltpu
from jax.sharding import PartitionSpec as P

STEP = 100
GRID = {64: (2, 4, 8), 8: (2, 2, 2)}
RY, RX, RZ = 32, 32, 16
F32 = jnp.float32
WIRE = jnp.float32
BF16 = jnp.bfloat16


def kernel(
    nl, ny, nx, nz,
    hid, lat, ids, old,
    update, new_logw,
    hv, ys, xs, zs, yr, xr, zr, y2s, x2s, z2s, y2r, x2r, z2r, y3s, x3s, z3s, y3r, x3r, z3r,
    high, low, oh, ar,
    hsem, ysend, yrecv, xsend, xrecv, zsend, zrecv,
    y2send, y2recv, x2send, x2recv, z2send, z2recv,
    y3send, y3recv, x3send, x3recv, z3send, z3recv,
    gsend, grecv, lsend, lrecv, osend, orecv, asend, arecv,
):
    g = lax.axis_index("language")
    f = lax.axis_index("fsdp")
    y = f // (nx * nz)
    x = (f // nz) % nx
    z = f % nz
    ranks = lat.shape[1]
    toks = hid.shape[1]
    cols = 2 * ranks
    blk = hid.shape[2] // (ny * nx)

    def at(yy, xx, zz):
        return {"fsdp": (yy * nx + xx) * nz + zz, "language": g}

    def lang(gg):
        return {"fsdp": f, "language": gg}

    def hop(v, d, n):
        return lax.rem(v + d, n)

    zpeers = [at(y, x, hop(z, d, nz)) for d in range(1, nz)]
    xpeers = [at(y, hop(x, d, nx), z) for d in range(1, nx)]
    ypeer = at(1 - y, x, z)
    lpeers = [lang(hop(g, d, nl)) for d in range(1, nl)]
    peers = [ypeer] + xpeers + zpeers + lpeers

    barrier = pltpu.get_barrier_semaphore()
    for p in peers:
        pl.semaphore_signal(barrier, inc=1, device_id=p, device_id_type=pl.DeviceIdType.MESH)

    def send(src, dst, ssem, rsem, dev, keep=True):
        c = pltpu.make_async_remote_copy(
            src_ref=src, dst_ref=dst, send_sem=ssem, recv_sem=rsem,
            device_id=dev, device_id_type=pl.DeviceIdType.MESH,
        )
        c.start()
        if keep:
            sent.append(c)

    def wait(dst, rsem):
        pltpu.make_async_copy(dst, dst, rsem).wait()

    sent = []
    xorder = [2, 1, 3, 0] if nx == 4 else list(range(1, nx)) + [0]
    order = [(dy, dx) for dy in (1, 0) for dx in xorder]
    loads = []
    for i, (dy, dx) in enumerate(order):
        c = hop(y, dy, ny) * nx + hop(x, dx, nx)
        at0 = c * blk
        if blk % 128 == 0:
            at0 = pl.multiple_of(at0, 128)
        cp = pltpu.make_async_copy(hid.at[:, :, pl.ds(at0, blk)], hv.at[i], hsem.at[i])
        cp.start()
        loads.append(cp)

    lane = lax.broadcasted_iota(jnp.int32, (1, 128), 1)
    row = lax.broadcasted_iota(jnp.int32, (2, 128), 0)
    lane2 = lax.broadcasted_iota(jnp.int32, (2, 128), 1)
    mine = jnp.where(row == 0, ids[0], ids[1])
    oh[g] = (mine == lane2).astype(F32)
    weights_old = jnp.ones((1, 128), F32)
    for k in range(old.shape[0]):
        weights_old = jnp.where(lane == k, old[k], weights_old)

    zero = jnp.zeros((ranks, toks), jnp.bfloat16)
    lhs = jnp.concatenate(
        [jnp.concatenate([lat[0], zero], axis=1), jnp.concatenate([zero, lat[1]], axis=1)], axis=0
    )

    for i, (dy, dx) in enumerate(order):
        yy, xx = hop(y, dy, ny), hop(x, dx, nx)
        loads[i].wait()
        rhs = hv[i].reshape(2 * toks, blk)
        part = jnp.dot(lhs, rhs, preferred_element_type=F32)
        part = part.T.reshape(nz, RY + RX + RZ, cols).astype(WIRE)
        ys[yy, xx] = part[:, :RY]
        xs[xx, yy] = part[:, RY : RY + RX]
        zs[:, yy, xx] = part[:, RY + RX :]
        if i == 0:
            pl.semaphore_wait(barrier, len(peers))
        if dy:
            send(ys.at[yy, xx], yr.at[xx], ysend.at[dx], yrecv.at[dx], ypeer)
        if dx:
            send(xs.at[xx, yy], xr.at[dx - 1, yy], xsend.at[dx - 1, dy], xrecv.at[dx - 1, dy], xpeers[dx - 1])
    for d in range(1, nz):
        send(zs.at[hop(z, d, nz)], zr.at[d - 1], zsend.at[d - 1], zrecv.at[d - 1], zpeers[d - 1])
    for d in range(1, nl):
        send(oh.at[g], oh.at[g], osend.at[d - 1], orecv.at[d - 1], lpeers[d - 1])

    for dx in xorder:
        xx = hop(x, dx, nx)
        wait(yr.at[xx], yrecv.at[dx])
        y2s[xx] = (ys[y, xx].astype(F32) + yr[xx].astype(F32)).astype(WIRE)
        if dx:
            send(y2s.at[xx], y2r.at[dx - 1], y2send.at[dx - 1], y2recv.at[dx - 1], xpeers[dx - 1])
    for dy in (1, 0):
        yy = hop(y, dy, ny)
        acc = xs[x, yy].astype(F32)
        for d in range(1, nx):
            wait(xr.at[d - 1, yy], xrecv.at[d - 1, dy])
            acc = acc + xr[d - 1, yy].astype(F32)
        x2s[yy] = acc.astype(WIRE)
        if dy:
            send(x2s.at[yy], x2r, x2send, x2recv, ypeer)
    acc = zs[z].astype(F32)
    for d in range(1, nz):
        wait(zr.at[d - 1], zrecv.at[d - 1])
        acc = acc + zr[d - 1].astype(F32)
    z2s[...] = acc.astype(WIRE)
    send(z2s.at[1 - y], z2r, z2send, z2recv, ypeer)

    wait(x2r, x2recv)
    x3s[...] = (x2s[y].astype(F32) + x2r[...].astype(F32)).astype(WIRE)
    for d in range(1, nz):
        send(x3s.at[hop(z, d, nz)], x3r.at[d - 1], x3send.at[d - 1], x3recv.at[d - 1], zpeers[d - 1])
    acc = y2s[x].astype(F32)
    for d in range(1, nx):
        wait(y2r.at[d - 1], y2recv.at[d - 1])
        acc = acc + y2r[d - 1].astype(F32)
    y3s[...] = acc.astype(WIRE)
    for d in range(1, nz):
        send(y3s.at[hop(z, d, nz)], y3r.at[d - 1], y3send.at[d - 1], y3recv.at[d - 1], zpeers[d - 1])
    wait(z2r, z2recv)
    z3s[...] = (z2s[y].astype(F32) + z2r[...].astype(F32)).astype(WIRE)
    for d in range(1, nx):
        send(z3s.at[hop(x, d, nx)], z3r.at[d - 1], z3send.at[d - 1], z3recv.at[d - 1], xpeers[d - 1])

    parts = ((0, RY), (RY, RX), (RY + RX, RZ))

    def finish(own, r, rsem, n, part):
        lo, size = parts[part]
        acc = own.astype(F32)
        for d in range(1, n):
            wait(r.at[d - 1], rsem.at[d - 1])
            acc = acc + r[d - 1].astype(F32)
        top = acc.astype(BF16)
        high[g, lo : lo + size] = top
        low[g, lo : lo + size] = (acc - top.astype(F32)).astype(BF16)
        for d in range(1, nl):
            ref = high.at[g, pl.ds(lo, size)]
            send(ref, ref, gsend.at[part, d - 1], grecv.at[part, d - 1], lpeers[d - 1])

    finish(x3s[z], x3r, x3recv, nz, 1)
    finish(z3s[x], z3r, z3recv, nx, 2)
    finish(y3s[z], y3r, y3recv, nz, 0)
    for d in range(1, nl):
        send(low.at[g], low.at[g], lsend.at[d - 1], lrecv.at[d - 1], lpeers[d - 1])

    for d in range(1, nl):
        src = hop(g, nl - d, nl)
        wait(oh.at[src], orecv.at[d - 1])
        for part, (lo, size) in enumerate(parts):
            wait(high.at[src, pl.ds(lo, size)], grecv.at[part, d - 1])

    slots = high[...].astype(F32)
    total = jnp.sum(slots, axis=0)
    both = total + pltpu.roll(total, ranks, 1)
    prods = jnp.sum(slots * both[None], axis=1)
    first_slot = lane < ranks
    dot0 = jnp.sum(jnp.where(first_slot, prods, 0.0), axis=1, keepdims=True)
    dot1 = jnp.sum(jnp.where(first_slot, 0.0, prods), axis=1, keepdims=True)
    square = jnp.sum(jnp.where(first_slot, jnp.sum(both * both, axis=0, keepdims=True), 0.0), axis=1, keepdims=True)
    oh0, oh1 = oh[:, 0, :], oh[:, 1, :]
    vec = jnp.sum(oh0 * dot0 + oh1 * dot1, axis=0, keepdims=True)
    langs = old.shape[0]
    vec = jnp.where(lane == langs, square, vec)

    ar[f] = vec
    n = ny * nx * nz
    for d in range(1, n):
        yy, xx, zz = hop(y, d // (nx * nz), ny), hop(x, d // nz % nx, nx), hop(z, d % nz, nz)
        send(ar.at[f], ar.at[f], asend, arecv, at(yy, xx, zz), False)
    wait(ar.at[pl.ds(0, n - 1)], arecv)
    vec = jnp.sum(ar[...], axis=0)

    square = jnp.sum(jnp.where(lane == langs, vec, 0.0), axis=1, keepdims=True) + 1e-06
    valid = lane < langs
    logits = jnp.log(weights_old) + langs * (jnp.where(valid, vec, 0.0) / square)
    norm = jnp.log(jnp.sum(jnp.where(valid, jnp.exp(logits), 0.0), axis=1, keepdims=True))
    logw = logits - norm
    new_logw[...] = logw
    weights = jnp.where(valid, jnp.exp(logw), 0.0)
    w0 = jnp.sum(oh0 * weights, axis=1, keepdims=True)
    w1 = jnp.sum(oh1 * weights, axis=1, keepdims=True)
    slot_weight = jnp.where(first_slot, w0, w1)
    for d in range(1, nl):
        wait(low.at[hop(g, nl - d, nl)], lrecv.at[d - 1])
    slots = slots + low[...].astype(F32)
    total = jnp.sum(slots * slot_weight[:, None, :], axis=0).T
    update[...] = total[:ranks] + total[ranks:]

    for c in sent:
        c.wait_send()
    pltpu.make_async_copy(ar.at[pl.ds(0, n - 1)], ar.at[pl.ds(0, n - 1)], asend).wait()


def adamw(grad, logw, param, first, second, new_param, new_first, new_second, new_logw):
    update = grad[...]
    m = 0.9 * first[...] + 0.1 * update
    v = 0.95 * second[...] + 0.05 * update * update
    new_first[...] = m
    new_second[...] = v
    m_hat = m / (1.0 - 0.9**STEP)
    v_hat = v / (1.0 - 0.95**STEP)
    p = param[...]
    new_param[...] = p - 0.02 * (m_hat / (jnp.sqrt(v_hat) + 1e-08) + 0.1 * p)
    new_logw[...] = logw[0, : new_logw.shape[0]]


def local(nl, ny, nx, nz, hidden, latent_grad, lang_ids, old_weights, param, first_moment, second_moment):
    rows, ranks = param.shape
    cols = 2 * ranks
    assert rows == RY + RX + RZ and hidden.shape[0] == 2
    blk = hidden.shape[2] // (ny * nx)
    vmem = pl.BlockSpec(memory_space=pltpu.VMEM)
    smem = pl.BlockSpec(memory_space=pltpu.SMEM)
    dma = pltpu.SemaphoreType.DMA
    b = lambda *s: pltpu.VMEM(s + (cols,), WIRE)
    mat = jax.ShapeDtypeStruct((ranks, rows), F32)
    scratch = [
        pltpu.VMEM((ny * nx, 2, hidden.shape[1], blk), jnp.bfloat16),
        b(ny, nx, nz, RY), b(nx, ny, nz, RX), b(nz, ny, nx, RZ),
        b(nx, nz, RY), b(nx - 1, ny, nz, RX), b(nz - 1, ny, nx, RZ),
        b(nx, nz, RY), b(ny, nz, RX), b(ny, nx, RZ),
        b(nx - 1, nz, RY), b(nz, RX), b(nx, RZ),
        b(nz, RY), b(nz, RX), b(nx, RZ),
        b(nz - 1, RY), b(nz - 1, RX), b(nx - 1, RZ),
        pltpu.VMEM((nl, rows, cols), BF16), pltpu.VMEM((nl, rows, cols), BF16),
        pltpu.VMEM((nl, 2, 128), F32),
        pltpu.VMEM((ny * nx * nz, 1, 128), F32),
        dma((ny * nx,)),
        dma((nx,)), dma((nx,)), dma((nx - 1, ny)), dma((nx - 1, ny)), dma((nz - 1,)), dma((nz - 1,)),
        dma((nx - 1,)), dma((nx - 1,)), dma, dma, dma, dma,
        dma((nz - 1,)), dma((nz - 1,)), dma((nz - 1,)), dma((nz - 1,)), dma((nx - 1,)), dma((nx - 1,)),
        dma((3, nl - 1)), dma((3, nl - 1)), dma((nl - 1,)), dma((nl - 1,)),
        dma((nl - 1,)), dma((nl - 1,)), dma, dma,
    ]
    update, logw = pl.pallas_call(
        functools.partial(kernel, nl, ny, nx, nz),
        out_shape=(mat, jax.ShapeDtypeStruct((1, 128), F32)),
        in_specs=[pl.BlockSpec(memory_space=pl.ANY), vmem, smem, smem],
        out_specs=(vmem, vmem),
        scratch_shapes=scratch,
        compiler_params=pltpu.CompilerParams(
            collective_id=0, has_side_effects=True, vmem_limit_bytes=61 * 1024 * 1024
        ),
        name="reweight",
    )(hidden, latent_grad.transpose(0, 2, 1), lang_ids, old_weights)
    outs = pl.pallas_call(
        adamw,
        out_shape=(mat, mat, mat, jax.ShapeDtypeStruct(old_weights.shape, F32)),
        in_specs=[vmem] * 5,
        out_specs=(vmem,) * 4,
        name="adamw",
    )(update, logw, param.T, first_moment.T, second_moment.T)
    return (outs[0].T, outs[1].T, outs[2].T, outs[3])


def solution(mesh):
    nl = mesh.shape["language"]
    ny, nx, nz = GRID[mesh.shape["fsdp"]]
    placed = (
        P("language", "fsdp", None),
        P("language", "fsdp", None),
        P("language"),
        P(),
        P("fsdp", None),
        P("fsdp", None),
        P("fsdp", None),
    )
    return jax.shard_map(
        functools.partial(local, nl, ny, nx, nz),
        mesh=mesh,
        in_specs=placed,
        out_specs=(P("fsdp", None), P("fsdp", None), P("fsdp", None), P()),
        check_vma=False,
    )
```

```python
import functools

import jax
import jax.numpy as jnp
from jax import lax
from jax.experimental import pallas as pl
from jax.experimental.pallas import tpu as pltpu
from jax.sharding import PartitionSpec as P

STEP = 100
GRID = {64: (2, 4, 8), 8: (2, 2, 2)}
RY, RX, RZ = 32, 32, 16
F32 = jnp.float32
BF16 = jnp.bfloat16
ORDER = ((1, 0), (2, 0), (1, 1), (3, 0), (2, 1), (3, 1))


def kernel(
    nl, ny, nx, nz,
    hid, lat, ids, old,
    update, new_logw,
    hv, ys, xs, zs, yr, xr, zr, y2s, x2s, z2s, y2r, x2r, z2r, y3s, x3s, z3s, y3r, x3r, z3r,
    both, oh, ar,
    hsem, ysend, yrecv, xsend, xrecv, zsend, zrecv,
    y2send, y2recv, x2send, x2recv, z2send, z2recv,
    y3send, y3recv, x3send, x3recv, z3send, z3recv,
    gsend, grecv, lsend, lrecv, osend, orecv, asend, arecv,
):
    g = lax.axis_index("language")
    f = lax.axis_index("fsdp")
    y = f // (nx * nz)
    x = (f // nz) % nx
    z = f % nz
    ranks = lat.shape[1]
    toks = hid.shape[1]
    cols = 2 * ranks
    blk = hid.shape[2] // (ny * nx)

    def at(yy, xx, zz):
        return {"fsdp": (yy * nx + xx) * nz + zz, "language": g}

    def lang(gg):
        return {"fsdp": f, "language": gg}

    def hop(v, d, n):
        return lax.rem(v + d, n)

    zpeers = [at(y, x, hop(z, d, nz)) for d in range(1, nz)]
    xpeers = [at(y, hop(x, d, nx), z) for d in range(1, nx)]
    ypeer = at(1 - y, x, z)
    lpeers = [lang(hop(g, d, nl)) for d in range(1, nl)]
    peers = [ypeer] + xpeers + zpeers + lpeers

    barrier = pltpu.get_barrier_semaphore()
    for p in peers:
        pl.semaphore_signal(barrier, inc=1, device_id=p, device_id_type=pl.DeviceIdType.MESH)

    def send(src, dst, ssem, rsem, dev, keep=True):
        c = pltpu.make_async_remote_copy(
            src_ref=src, dst_ref=dst, send_sem=ssem, recv_sem=rsem,
            device_id=dev, device_id_type=pl.DeviceIdType.MESH,
        )
        c.start()
        if keep:
            sent.append(c)

    def wait(dst, rsem):
        pltpu.make_async_copy(dst, dst, rsem).wait()

    sent = []
    xorder = [2, 1, 3, 0] if nx == 4 else list(range(1, nx)) + [0]
    order = [(dy, dx) for dy in (1, 0) for dx in xorder]
    loads = []
    for i, (dy, dx) in enumerate(order):
        c = hop(y, dy, ny) * nx + hop(x, dx, nx)
        at0 = c * blk
        if blk % 128 == 0:
            at0 = pl.multiple_of(at0, 128)
        cp = pltpu.make_async_copy(hid.at[:, :, pl.ds(at0, blk)], hv.at[i], hsem.at[i])
        cp.start()
        loads.append(cp)

    lane = lax.broadcasted_iota(jnp.int32, (1, 128), 1)
    row = lax.broadcasted_iota(jnp.int32, (2, 128), 0)
    lane2 = lax.broadcasted_iota(jnp.int32, (2, 128), 1)
    mine = jnp.where(row == 0, ids[0], ids[1])
    oh[g] = (mine == lane2).astype(F32)
    weights_old = jnp.ones((1, 128), F32)
    for k in range(old.shape[0]):
        weights_old = jnp.where(lane == k, old[k], weights_old)

    zero = jnp.zeros((ranks, toks), jnp.bfloat16)
    lhs = jnp.concatenate(
        [jnp.concatenate([lat[0], zero], axis=1), jnp.concatenate([zero, lat[1]], axis=1)], axis=0
    )

    def split(value):
        high = value.astype(BF16)
        return high, (value - high.astype(F32)).astype(BF16)

    def put(k, dst, terms):
        total = terms[0].astype(F32)
        for term in terms[1:]:
            total = total + term.astype(F32)
        if k == 0:
            dst(0)[...], dst(1)[...] = split(total)
        else:
            dst(1)[...] = (total + dst(1)[...].astype(F32)).astype(BF16)

    def first_sends(k, dy, dx):
        yy, xx = hop(y, dy, ny), hop(x, dx, nx)
        if dy:
            send(ys.at[k, yy, xx], yr.at[k, xx], ysend.at[k, dx], yrecv.at[k, dx], ypeer)
        if dx:
            send(
                xs.at[k, xx, yy], xr.at[k, dx - 1, yy], xsend.at[k, dx - 1, dy], xrecv.at[k, dx - 1, dy],
                xpeers[dx - 1],
            )

    def last_sends(k):
        for d in range(1, nz):
            send(zs.at[k, hop(z, d, nz)], zr.at[k, d - 1], zsend.at[k, d - 1], zrecv.at[k, d - 1], zpeers[d - 1])

    for i, (dy, dx) in enumerate(order):
        yy, xx = hop(y, dy, ny), hop(x, dx, nx)
        loads[i].wait()
        rhs = hv[i].reshape(2 * toks, blk)
        part = jnp.dot(lhs, rhs, preferred_element_type=F32)
        part = part.T.reshape(nz, RY + RX + RZ, cols)
        for k, half in enumerate(split(part)):
            ys[k, yy, xx] = half[:, :RY]
            xs[k, xx, yy] = half[:, RY : RY + RX]
            zs[k, :, yy, xx] = half[:, RY + RX :]
        if i == 0:
            pl.semaphore_wait(barrier, len(peers))
        first_sends(0, dy, dx)
    last_sends(0)
    for d in range(1, nl):
        send(oh.at[g], oh.at[g], osend.at[d - 1], orecv.at[d - 1], lpeers[d - 1])
    for dy, dx in order:
        first_sends(1, dy, dx)
    last_sends(1)

    def reduce1(k):
        for dx in xorder:
            xx = hop(x, dx, nx)
            wait(yr.at[k, xx], yrecv.at[k, dx])
            put(k, lambda j: y2s.at[j, xx], [ys[k, y, xx], yr[k, xx]])
            if dx:
                send(y2s.at[k, xx], y2r.at[k, dx - 1], y2send.at[k, dx - 1], y2recv.at[k, dx - 1], xpeers[dx - 1])
        for dy in (1, 0):
            yy = hop(y, dy, ny)
            for d in range(1, nx):
                wait(xr.at[k, d - 1, yy], xrecv.at[k, d - 1, dy])
            put(k, lambda j: x2s.at[j, yy], [xs[k, x, yy]] + [xr[k, d - 1, yy] for d in range(1, nx)])
            if dy:
                send(x2s.at[k, yy], x2r.at[k], x2send.at[k], x2recv.at[k], ypeer)
        for d in range(1, nz):
            wait(zr.at[k, d - 1], zrecv.at[k, d - 1])
        put(k, lambda j: z2s.at[j], [zs[k, z]] + [zr[k, d - 1] for d in range(1, nz)])
        send(z2s.at[k, 1 - y], z2r.at[k], z2send.at[k], z2recv.at[k], ypeer)

    def reduce2(k):
        wait(x2r.at[k], x2recv.at[k])
        put(k, lambda j: x3s.at[j], [x2s[k, y], x2r[k]])
        for d in range(1, nz):
            send(x3s.at[k, hop(z, d, nz)], x3r.at[k, d - 1], x3send.at[k, d - 1], x3recv.at[k, d - 1], zpeers[d - 1])
        for d in range(1, nx):
            wait(y2r.at[k, d - 1], y2recv.at[k, d - 1])
        put(k, lambda j: y3s.at[j], [y2s[k, x]] + [y2r[k, d - 1] for d in range(1, nx)])
        for d in range(1, nz):
            send(y3s.at[k, hop(z, d, nz)], y3r.at[k, d - 1], y3send.at[k, d - 1], y3recv.at[k, d - 1], zpeers[d - 1])
        wait(z2r.at[k], z2recv.at[k])
        put(k, lambda j: z3s.at[j], [z2s[k, y], z2r[k]])
        for d in range(1, nx):
            send(z3s.at[k, hop(x, d, nx)], z3r.at[k, d - 1], z3send.at[k, d - 1], z3recv.at[k, d - 1], xpeers[d - 1])

    parts = ((0, RY), (RY, RX), (RY + RX, RZ))

    def finish(k, own, r, rsem, n, part):
        lo, size = parts[part]
        for d in range(1, n):
            wait(r.at[k, d - 1], rsem.at[k, d - 1])
        put(k, lambda j: both.at[j, g, pl.ds(lo, size)], [own] + [r[k, d - 1] for d in range(1, n)])
        if k == 0:
            for d in range(1, nl):
                ref = both.at[0, g, pl.ds(lo, size)]
                send(ref, ref, gsend.at[part, d - 1], grecv.at[part, d - 1], lpeers[d - 1])

    def reduce3(k):
        finish(k, x3s[k, z], x3r, x3recv, nz, 1)
        finish(k, z3s[k, x], z3r, z3recv, nx, 2)
        finish(k, y3s[k, z], y3r, y3recv, nz, 0)
        if k == 1:
            for d in range(1, nl):
                send(both.at[1, g], both.at[1, g], lsend.at[d - 1], lrecv.at[d - 1], lpeers[d - 1])

    for stage, k in ORDER:
        (reduce1, reduce2, reduce3)[stage - 1](k)

    for d in range(1, nl):
        src = hop(g, nl - d, nl)
        wait(oh.at[src], orecv.at[d - 1])
        for part, (lo, size) in enumerate(parts):
            wait(both.at[0, src, pl.ds(lo, size)], grecv.at[part, d - 1])

    slots = both[0].astype(F32)
    total = jnp.sum(slots, axis=0)
    twice = total + pltpu.roll(total, ranks, 1)
    prods = jnp.sum(slots * twice[None], axis=1)
    first_slot = lane < ranks
    dot0 = jnp.sum(jnp.where(first_slot, prods, 0.0), axis=1, keepdims=True)
    dot1 = jnp.sum(jnp.where(first_slot, 0.0, prods), axis=1, keepdims=True)
    square = jnp.sum(jnp.where(first_slot, jnp.sum(twice * twice, axis=0, keepdims=True), 0.0), axis=1, keepdims=True)
    oh0, oh1 = oh[:, 0, :], oh[:, 1, :]
    vec = jnp.sum(oh0 * dot0 + oh1 * dot1, axis=0, keepdims=True)
    langs = old.shape[0]
    vec = jnp.where(lane == langs, square, vec)

    ar[f] = vec
    n = ny * nx * nz
    for d in range(1, n):
        yy, xx, zz = hop(y, d // (nx * nz), ny), hop(x, d // nz % nx, nx), hop(z, d % nz, nz)
        send(ar.at[f], ar.at[f], asend, arecv, at(yy, xx, zz), False)
    wait(ar.at[pl.ds(0, n - 1)], arecv)
    vec = jnp.sum(ar[...], axis=0)

    square = jnp.sum(jnp.where(lane == langs, vec, 0.0), axis=1, keepdims=True) + 1e-06
    valid = lane < langs
    logits = jnp.log(weights_old) + langs * (jnp.where(valid, vec, 0.0) / square)
    norm = jnp.log(jnp.sum(jnp.where(valid, jnp.exp(logits), 0.0), axis=1, keepdims=True))
    logw = logits - norm
    new_logw[...] = logw
    weights = jnp.where(valid, jnp.exp(logw), 0.0)
    w0 = jnp.sum(oh0 * weights, axis=1, keepdims=True)
    w1 = jnp.sum(oh1 * weights, axis=1, keepdims=True)
    slot_weight = jnp.where(first_slot, w0, w1)
    for d in range(1, nl):
        wait(both.at[1, hop(g, nl - d, nl)], lrecv.at[d - 1])
    slots = slots + both[1].astype(F32)
    total = jnp.sum(slots * slot_weight[:, None, :], axis=0).T
    update[...] = total[:ranks] + total[ranks:]

    for c in sent:
        c.wait_send()
    pltpu.make_async_copy(ar.at[pl.ds(0, n - 1)], ar.at[pl.ds(0, n - 1)], asend).wait()


def adamw(grad, logw, param, first, second, new_param, new_first, new_second, new_logw):
    update = grad[...]
    m = 0.9 * first[...] + 0.1 * update
    v = 0.95 * second[...] + 0.05 * update * update
    new_first[...] = m
    new_second[...] = v
    m_hat = m / (1.0 - 0.9**STEP)
    v_hat = v / (1.0 - 0.95**STEP)
    p = param[...]
    new_param[...] = p - 0.02 * (m_hat / (jnp.sqrt(v_hat) + 1e-08) + 0.1 * p)
    new_logw[...] = logw[0, : new_logw.shape[0]]


def local(nl, ny, nx, nz, hidden, latent_grad, lang_ids, old_weights, param, first_moment, second_moment):
    rows, ranks = param.shape
    cols = 2 * ranks
    assert rows == RY + RX + RZ and hidden.shape[0] == 2
    blk = hidden.shape[2] // (ny * nx)
    vmem = pl.BlockSpec(memory_space=pltpu.VMEM)
    smem = pl.BlockSpec(memory_space=pltpu.SMEM)
    dma = pltpu.SemaphoreType.DMA
    b = lambda *s: pltpu.VMEM((2,) + s + (cols,), BF16)
    dma2 = lambda *s: dma((2,) + s)
    mat = jax.ShapeDtypeStruct((ranks, rows), F32)
    scratch = [
        pltpu.VMEM((ny * nx, 2, hidden.shape[1], blk), jnp.bfloat16),
        b(ny, nx, nz, RY), b(nx, ny, nz, RX), b(nz, ny, nx, RZ),
        b(nx, nz, RY), b(nx - 1, ny, nz, RX), b(nz - 1, ny, nx, RZ),
        b(nx, nz, RY), b(ny, nz, RX), b(ny, nx, RZ),
        b(nx - 1, nz, RY), b(nz, RX), b(nx, RZ),
        b(nz, RY), b(nz, RX), b(nx, RZ),
        b(nz - 1, RY), b(nz - 1, RX), b(nx - 1, RZ),
        b(nl, rows),
        pltpu.VMEM((nl, 2, 128), F32),
        pltpu.VMEM((ny * nx * nz, 1, 128), F32),
        dma((ny * nx,)),
        dma2(nx), dma2(nx), dma2(nx - 1, ny), dma2(nx - 1, ny), dma2(nz - 1), dma2(nz - 1),
        dma2(nx - 1), dma2(nx - 1), dma2(), dma2(), dma2(), dma2(),
        dma2(nz - 1), dma2(nz - 1), dma2(nz - 1), dma2(nz - 1), dma2(nx - 1), dma2(nx - 1),
        dma((3, nl - 1)), dma((3, nl - 1)), dma((nl - 1,)), dma((nl - 1,)), dma((nl - 1,)), dma((nl - 1,)),
        dma, dma,
    ]
    update, logw = pl.pallas_call(
        functools.partial(kernel, nl, ny, nx, nz),
        out_shape=(mat, jax.ShapeDtypeStruct((1, 128), F32)),
        in_specs=[pl.BlockSpec(memory_space=pl.ANY), vmem, smem, smem],
        out_specs=(vmem, vmem),
        scratch_shapes=scratch,
        compiler_params=pltpu.CompilerParams(
            collective_id=0, has_side_effects=True, vmem_limit_bytes=61 * 1024 * 1024
        ),
        name="reweight",
    )(hidden, latent_grad.transpose(0, 2, 1), lang_ids, old_weights)
    outs = pl.pallas_call(
        adamw,
        out_shape=(mat, mat, mat, jax.ShapeDtypeStruct(old_weights.shape, F32)),
        in_specs=[vmem] * 5,
        out_specs=(vmem,) * 4,
        name="adamw",
    )(update, logw, param.T, first_moment.T, second_moment.T)
    return (outs[0].T, outs[1].T, outs[2].T, outs[3])


def solution(mesh):
    nl = mesh.shape["language"]
    ny, nx, nz = GRID[mesh.shape["fsdp"]]
    placed = (
        P("language", "fsdp", None),
        P("language", "fsdp", None),
        P("language"),
        P(),
        P("fsdp", None),
        P("fsdp", None),
        P("fsdp", None),
    )
    return jax.shard_map(
        functools.partial(local, nl, ny, nx, nz),
        mesh=mesh,
        in_specs=placed,
        out_specs=(P("fsdp", None), P("fsdp", None), P("fsdp", None), P()),
        check_vma=False,
    )
```

```python
import functools

import jax
import jax.numpy as jnp
from jax import lax
from jax.experimental import pallas as pl
from jax.experimental.pallas import tpu as pltpu
from jax.sharding import PartitionSpec as P

STEP = 100
GRID = {64: (2, 4, 8), 8: (2, 2, 2)}
RY, RX, RZ = 32, 32, 16
F32 = jnp.float32
BF16 = jnp.bfloat16
ORDER = (
    "y10", "lx", "x10", "z10", "x20", "y20", "z20", "y11", "z11", "x11", "x30", "z30", "y30",
    "x21", "y21", "z21",
)
LATE = ("x31", "z31", "y31")


def kernel(
    nl, ny, nx, nz,
    hid, lat, ids, old,
    update, new_logw,
    hv, ys, xs, zs, yr, xr, zr, y2s, x2s, z2s, y2r, x2r, z2r, y3s, x3s, z3s, y3r, x3r, z3r,
    both, oh, ar,
    hsem, ysend, yrecv, xsend, xrecv, zsend, zrecv,
    y2send, y2recv, x2send, x2recv, z2send, z2recv,
    y3send, y3recv, x3send, x3recv, z3send, z3recv,
    gsend, grecv, fsend, frecv, osend, orecv, asend, arecv,
):
    g = lax.axis_index("language")
    f = lax.axis_index("fsdp")
    y = f // (nx * nz)
    x = (f // nz) % nx
    z = f % nz
    ranks = lat.shape[1]
    toks = hid.shape[1]
    cols = 2 * ranks
    blk = hid.shape[2] // (ny * nx)

    def at(yy, xx, zz):
        return {"fsdp": (yy * nx + xx) * nz + zz, "language": g}

    def lang(gg):
        return {"fsdp": f, "language": gg}

    def hop(v, d, n):
        return lax.rem(v + d, n)

    zpeers = [at(y, x, hop(z, d, nz)) for d in range(1, nz)]
    xpeers = [at(y, hop(x, d, nx), z) for d in range(1, nx)]
    ypeer = at(1 - y, x, z)
    twin = g + 1 - 2 * (g % 2)
    lpeers = [lang(twin)] + [lang(hop(g, 2 * d, nl)) for d in range(1, nl // 2)]
    peers = [ypeer] + xpeers + zpeers + lpeers

    barrier = pltpu.get_barrier_semaphore()
    for p in peers:
        pl.semaphore_signal(barrier, inc=1, device_id=p, device_id_type=pl.DeviceIdType.MESH)

    def send(src, dst, ssem, rsem, dev, keep=True):
        c = pltpu.make_async_remote_copy(
            src_ref=src, dst_ref=dst, send_sem=ssem, recv_sem=rsem,
            device_id=dev, device_id_type=pl.DeviceIdType.MESH,
        )
        c.start()
        if keep:
            sent.append(c)

    def wait(dst, rsem):
        pltpu.make_async_copy(dst, dst, rsem).wait()

    sent = []
    xorder = [2, 1, 3, 0] if nx == 4 else list(range(1, nx)) + [0]
    order = [(dy, dx) for dy in (1, 0) for dx in xorder]
    loads = []
    for i, (dy, dx) in enumerate(order):
        c = hop(y, dy, ny) * nx + hop(x, dx, nx)
        at0 = c * blk
        if blk % 128 == 0:
            at0 = pl.multiple_of(at0, 128)
        cp = pltpu.make_async_copy(hid.at[:, :, pl.ds(at0, blk)], hv.at[i], hsem.at[i])
        cp.start()
        loads.append(cp)

    lane = lax.broadcasted_iota(jnp.int32, (1, 128), 1)
    row = lax.broadcasted_iota(jnp.int32, (2, 128), 0)
    lane2 = lax.broadcasted_iota(jnp.int32, (2, 128), 1)
    mine = jnp.where(row == 0, ids[0], ids[1])
    oh[g] = (mine == lane2).astype(F32)
    weights_old = jnp.ones((1, 128), F32)
    for k in range(old.shape[0]):
        weights_old = jnp.where(lane == k, old[k], weights_old)

    zero = jnp.zeros((ranks, toks), jnp.bfloat16)
    lhs = jnp.concatenate(
        [jnp.concatenate([lat[0], zero], axis=1), jnp.concatenate([zero, lat[1]], axis=1)], axis=0
    )

    def split(value):
        high = value.astype(BF16)
        return high, (value - high.astype(F32)).astype(BF16)

    def put(k, dst, terms):
        total = terms[0].astype(F32)
        for term in terms[1:]:
            total = total + term.astype(F32)
        if k == 0:
            dst(0)[...], dst(1)[...] = split(total)
        else:
            dst(1)[...] = (total + dst(1)[...].astype(F32)).astype(BF16)

    def first_sends(k, dy, dx, do_y=True, do_x=True):
        yy, xx = hop(y, dy, ny), hop(x, dx, nx)
        if dy and do_y:
            send(ys.at[k, yy, xx], yr.at[k, xx], ysend.at[k, dx], yrecv.at[k, dx], ypeer)
        if dx and do_x:
            send(
                xs.at[k, xx, yy], xr.at[k, dx - 1, yy], xsend.at[k, dx - 1, dy], xrecv.at[k, dx - 1, dy],
                xpeers[dx - 1],
            )

    def last_sends(k):
        for d in range(1, nz):
            send(zs.at[k, hop(z, d, nz)], zr.at[k, d - 1], zsend.at[k, d - 1], zrecv.at[k, d - 1], zpeers[d - 1])

    for i, (dy, dx) in enumerate(order):
        yy, xx = hop(y, dy, ny), hop(x, dx, nx)
        loads[i].wait()
        rhs = hv[i].reshape(2 * toks, blk)
        part = jnp.dot(lhs, rhs, preferred_element_type=F32)
        part = part.T.reshape(nz, RY + RX + RZ, cols)
        for k, half in enumerate(split(part)):
            ys[k, yy, xx] = half[:, :RY]
            xs[k, xx, yy] = half[:, RY : RY + RX]
            zs[k, :, yy, xx] = half[:, RY + RX :]
        if i == 0:
            pl.semaphore_wait(barrier, len(peers))
        first_sends(0, dy, dx)
    last_sends(0)
    for d, p in enumerate(lpeers):
        send(oh.at[g], oh.at[g], osend.at[d], orecv.at[d], p)
    last_sends(1)
    for dy, dx in order:
        first_sends(1, dy, dx, do_x=False)

    def first_y(k):
        for dx in xorder:
            xx = hop(x, dx, nx)
            wait(yr.at[k, xx], yrecv.at[k, dx])
            put(k, lambda j: y2s.at[j, xx], [ys[k, y, xx], yr[k, xx]])
            if dx:
                send(y2s.at[k, xx], y2r.at[k, dx - 1], y2send.at[k, dx - 1], y2recv.at[k, dx - 1], xpeers[dx - 1])

    def first_x(k):
        for dy in (1, 0):
            yy = hop(y, dy, ny)
            for d in range(1, nx):
                wait(xr.at[k, d - 1, yy], xrecv.at[k, d - 1, dy])
            put(k, lambda j: x2s.at[j, yy], [xs[k, x, yy]] + [xr[k, d - 1, yy] for d in range(1, nx)])
            if dy:
                send(x2s.at[k, yy], x2r.at[k], x2send.at[k], x2recv.at[k], ypeer)

    def first_z(k):
        for d in range(1, nz):
            wait(zr.at[k, d - 1], zrecv.at[k, d - 1])
        put(k, lambda j: z2s.at[j], [zs[k, z]] + [zr[k, d - 1] for d in range(1, nz)])
        send(z2s.at[k, 1 - y], z2r.at[k], z2send.at[k], z2recv.at[k], ypeer)

    def second_x(k):
        wait(x2r.at[k], x2recv.at[k])
        put(k, lambda j: x3s.at[j], [x2s[k, y], x2r[k]])
        for d in range(1, nz):
            send(x3s.at[k, hop(z, d, nz)], x3r.at[k, d - 1], x3send.at[k, d - 1], x3recv.at[k, d - 1], zpeers[d - 1])

    def second_y(k):
        for d in range(1, nx):
            wait(y2r.at[k, d - 1], y2recv.at[k, d - 1])
        put(k, lambda j: y3s.at[j], [y2s[k, x]] + [y2r[k, d - 1] for d in range(1, nx)])
        for d in range(1, nz):
            send(y3s.at[k, hop(z, d, nz)], y3r.at[k, d - 1], y3send.at[k, d - 1], y3recv.at[k, d - 1], zpeers[d - 1])

    def second_z(k):
        wait(z2r.at[k], z2recv.at[k])
        put(k, lambda j: z3s.at[j], [z2s[k, y], z2r[k]])
        for d in range(1, nx):
            send(z3s.at[k, hop(x, d, nx)], z3r.at[k, d - 1], z3send.at[k, d - 1], z3recv.at[k, d - 1], xpeers[d - 1])

    parts = ((0, RY), (RY, RX), (RY + RX, RZ))
    chips = nl // 2

    def third(k, own, r, rsem, n, part):
        lo, size = parts[part]
        for d in range(1, n):
            wait(r.at[k, d - 1], rsem.at[k, d - 1])
        put(k, lambda j: both.at[j, g, pl.ds(lo, size)], [own] + [r[k, d - 1] for d in range(1, n)])
        ref = both.at[k, g, pl.ds(lo, size)]
        for d, p in enumerate(lpeers):
            send(ref, ref, gsend.at[k, part, d], grecv.at[k, part, d], p)

    def third_x(k):
        third(k, x3s[k, z], x3r, x3recv, nz, 1)

    def third_z(k):
        third(k, z3s[k, x], z3r, z3recv, nx, 2)

    def third_y(k):
        third(k, y3s[k, z], y3r, y3recv, nz, 0)

    def low_x(k):
        for dy, dx in order:
            first_sends(1, dy, dx, do_y=False)

    def hand_over(k):
        for d in range(1, chips):
            src = hop(g, nl - 2 * d, nl)
            for part, (lo, size) in enumerate(parts):
                wait(both.at[k, src, pl.ds(lo, size)], grecv.at[k, part, d])
            send(both.at[k, src], both.at[k, src], fsend.at[k, d - 1], frecv.at[k, d - 1], lpeers[0])
            if k == 0:
                wait(oh.at[src], orecv.at[d])
                send(oh.at[src], oh.at[src], osend.at[chips + d - 1], orecv.at[chips + d - 1], lpeers[0])

    def take_over(k):
        for part, (lo, size) in enumerate(parts):
            wait(both.at[k, twin, pl.ds(lo, size)], grecv.at[k, part, 0])
        if k == 0:
            wait(oh.at[twin], orecv.at[0])
        for d in range(1, chips):
            src = hop(twin, nl - 2 * d, nl)
            wait(both.at[k, src], frecv.at[k, d - 1])
            if k == 0:
                wait(oh.at[src], orecv.at[chips + d - 1])

    steps = dict(
        y1=first_y, x1=first_x, z1=first_z, x2=second_x, y2=second_y, z2=second_z,
        x3=third_x, y3=third_y, z3=third_z, lx=low_x,
    )
    for step in ORDER:
        steps[step[:2]](int(step[2:] or 0))

    hand_over(0)
    for step in LATE:
        steps[step[:2]](int(step[2:] or 0))
    take_over(0)

    slots = both[0].astype(F32)
    total = jnp.sum(slots, axis=0)
    twice = total + pltpu.roll(total, ranks, 1)
    prods = jnp.sum(slots * twice[None], axis=1)
    first_slot = lane < ranks
    dot0 = jnp.sum(jnp.where(first_slot, prods, 0.0), axis=1, keepdims=True)
    dot1 = jnp.sum(jnp.where(first_slot, 0.0, prods), axis=1, keepdims=True)
    square = jnp.sum(jnp.where(first_slot, jnp.sum(twice * twice, axis=0, keepdims=True), 0.0), axis=1, keepdims=True)
    oh0, oh1 = oh[:, 0, :], oh[:, 1, :]
    vec = jnp.sum(oh0 * dot0 + oh1 * dot1, axis=0, keepdims=True)
    langs = old.shape[0]
    vec = jnp.where(lane == langs, square, vec)

    ar[f] = vec
    n = ny * nx * nz

    def far(d):
        dy, dx, dz = d // (nx * nz), d // nz % nx, d % nz
        return dy + min(dx, nx - dx) + min(dz, nz - dz)

    for d in sorted(range(1, n), key=lambda d: -far(d)):
        yy, xx, zz = hop(y, d // (nx * nz), ny), hop(x, d // nz % nx, nx), hop(z, d % nz, nz)
        send(ar.at[f], ar.at[f], asend, arecv, at(yy, xx, zz), False)
    hand_over(1)
    wait(ar.at[pl.ds(0, n - 1)], arecv)
    vec = jnp.sum(ar[...], axis=0)

    square = jnp.sum(jnp.where(lane == langs, vec, 0.0), axis=1, keepdims=True) + 1e-06
    valid = lane < langs
    logits = jnp.log(weights_old) + langs * (jnp.where(valid, vec, 0.0) / square)
    norm = jnp.log(jnp.sum(jnp.where(valid, jnp.exp(logits), 0.0), axis=1, keepdims=True))
    logw = logits - norm
    new_logw[...] = logw
    weights = jnp.where(valid, jnp.exp(logw), 0.0)
    w0 = jnp.sum(oh0 * weights, axis=1, keepdims=True)
    w1 = jnp.sum(oh1 * weights, axis=1, keepdims=True)
    slot_weight = jnp.where(first_slot, w0, w1)
    take_over(1)
    slots = slots + both[1].astype(F32)
    total = jnp.sum(slots * slot_weight[:, None, :], axis=0).T
    update[...] = total[:ranks] + total[ranks:]

    for c in sent:
        c.wait_send()
    pltpu.make_async_copy(ar.at[pl.ds(0, n - 1)], ar.at[pl.ds(0, n - 1)], asend).wait()


def adamw(grad, logw, param, first, second, new_param, new_first, new_second, new_logw):
    update = grad[...]
    m = 0.9 * first[...] + 0.1 * update
    v = 0.95 * second[...] + 0.05 * update * update
    new_first[...] = m
    new_second[...] = v
    m_hat = m / (1.0 - 0.9**STEP)
    v_hat = v / (1.0 - 0.95**STEP)
    p = param[...]
    new_param[...] = p - 0.02 * (m_hat / (jnp.sqrt(v_hat) + 1e-08) + 0.1 * p)
    new_logw[...] = logw[0, : new_logw.shape[0]]


def local(nl, ny, nx, nz, hidden, latent_grad, lang_ids, old_weights, param, first_moment, second_moment):
    rows, ranks = param.shape
    cols = 2 * ranks
    assert rows == RY + RX + RZ and hidden.shape[0] == 2
    blk = hidden.shape[2] // (ny * nx)
    vmem = pl.BlockSpec(memory_space=pltpu.VMEM)
    smem = pl.BlockSpec(memory_space=pltpu.SMEM)
    dma = pltpu.SemaphoreType.DMA
    b = lambda *s: pltpu.VMEM((2,) + s + (cols,), BF16)
    dma2 = lambda *s: dma((2,) + s)
    mat = jax.ShapeDtypeStruct((ranks, rows), F32)
    scratch = [
        pltpu.VMEM((ny * nx, 2, hidden.shape[1], blk), jnp.bfloat16),
        b(ny, nx, nz, RY), b(nx, ny, nz, RX), b(nz, ny, nx, RZ),
        b(nx, nz, RY), b(nx - 1, ny, nz, RX), b(nz - 1, ny, nx, RZ),
        b(nx, nz, RY), b(ny, nz, RX), b(ny, nx, RZ),
        b(nx - 1, nz, RY), b(nz, RX), b(nx, RZ),
        b(nz, RY), b(nz, RX), b(nx, RZ),
        b(nz - 1, RY), b(nz - 1, RX), b(nx - 1, RZ),
        b(nl, rows),
        pltpu.VMEM((nl, 2, 128), F32),
        pltpu.VMEM((ny * nx * nz, 1, 128), F32),
        dma((ny * nx,)),
        dma2(nx), dma2(nx), dma2(nx - 1, ny), dma2(nx - 1, ny), dma2(nz - 1), dma2(nz - 1),
        dma2(nx - 1), dma2(nx - 1), dma2(), dma2(), dma2(), dma2(),
        dma2(nz - 1), dma2(nz - 1), dma2(nz - 1), dma2(nz - 1), dma2(nx - 1), dma2(nx - 1),
        dma2(3, nl // 2), dma2(3, nl // 2), dma2(max(nl // 2 - 1, 1)), dma2(max(nl // 2 - 1, 1)), dma((nl - 1,)), dma((nl - 1,)),
        dma, dma,
    ]
    update, logw = pl.pallas_call(
        functools.partial(kernel, nl, ny, nx, nz),
        out_shape=(mat, jax.ShapeDtypeStruct((1, 128), F32)),
        in_specs=[pl.BlockSpec(memory_space=pl.ANY), vmem, smem, smem],
        out_specs=(vmem, vmem),
        scratch_shapes=scratch,
        compiler_params=pltpu.CompilerParams(
            collective_id=0, has_side_effects=True, vmem_limit_bytes=61 * 1024 * 1024
        ),
        name="reweight",
    )(hidden, latent_grad.transpose(0, 2, 1), lang_ids, old_weights)
    outs = pl.pallas_call(
        adamw,
        out_shape=(mat, mat, mat, jax.ShapeDtypeStruct(old_weights.shape, F32)),
        in_specs=[vmem] * 5,
        out_specs=(vmem,) * 4,
        name="adamw",
    )(update, logw, param.T, first_moment.T, second_moment.T)
    return (outs[0].T, outs[1].T, outs[2].T, outs[3])


def solution(mesh):
    nl = mesh.shape["language"]
    ny, nx, nz = GRID[mesh.shape["fsdp"]]
    placed = (
        P("language", "fsdp", None),
        P("language", "fsdp", None),
        P("language"),
        P(),
        P("fsdp", None),
        P("fsdp", None),
        P("fsdp", None),
    )
    return jax.shard_map(
        functools.partial(local, nl, ny, nx, nz),
        mesh=mesh,
        in_specs=placed,
        out_specs=(P("fsdp", None), P("fsdp", None), P("fsdp", None), P()),
        check_vma=False,
    )
```

```python
import functools

import jax
import jax.numpy as jnp
from jax import lax
from jax.experimental import pallas as pl
from jax.experimental.pallas import tpu as pltpu
from jax.sharding import PartitionSpec as P

STEP = 100
GRID = {64: (2, 4, 8), 8: (2, 2, 2)}
RY, RX, RZ = 32, 32, 16
F32 = jnp.float32
BF16 = jnp.bfloat16
ORDER = (
    "y10", "lx", "x10", "z10", "x20", "y20", "z20", "y11", "z11", "x11", "x30", "z30", "y30",
    "x21", "y21", "z21",
)
LATE = ("x31", "z31", "y31")


def kernel(
    nl, ny, nx, nz,
    hid, lat, ids, old,
    update, new_logw,
    hv, ys, xs, zs, yr, xr, zr, y2s, x2s, z2s, y2r, x2r, z2r, y3s, x3s, z3s, y3r, x3r, z3r,
    both, oh, ar,
    hsem, ysend, yrecv, xsend, xrecv, zsend, zrecv,
    y2send, y2recv, x2send, x2recv, z2send, z2recv,
    y3send, y3recv, x3send, x3recv, z3send, z3recv,
    gsend, grecv, fsend, frecv, osend, orecv, asend, arecv,
):
    g = lax.axis_index("language")
    f = lax.axis_index("fsdp")
    y = f // (nx * nz)
    x = (f // nz) % nx
    z = f % nz
    ranks = lat.shape[1]
    toks = hid.shape[1]
    cols = 2 * ranks
    blk = hid.shape[2] // (ny * nx)

    def at(yy, xx, zz):
        return {"fsdp": (yy * nx + xx) * nz + zz, "language": g}

    def lang(gg):
        return {"fsdp": f, "language": gg}

    def hop(v, d, n):
        return lax.rem(v + d, n)

    zpeers = [at(y, x, hop(z, d, nz)) for d in range(1, nz)]
    xpeers = [at(y, hop(x, d, nx), z) for d in range(1, nx)]
    ypeer = at(1 - y, x, z)
    twin = g + 1 - 2 * (g % 2)
    lpeers = [lang(twin)] + [lang(hop(g, 2 * d, nl)) for d in range(1, nl // 2)]
    peers = [ypeer] + xpeers + zpeers + lpeers

    barrier = pltpu.get_barrier_semaphore()
    for p in peers:
        pl.semaphore_signal(barrier, inc=1, device_id=p, device_id_type=pl.DeviceIdType.MESH)

    def send(src, dst, ssem, rsem, dev, keep=True):
        c = pltpu.make_async_remote_copy(
            src_ref=src, dst_ref=dst, send_sem=ssem, recv_sem=rsem,
            device_id=dev, device_id_type=pl.DeviceIdType.MESH,
        )
        c.start()
        if keep:
            sent.append(c)

    def wait(dst, rsem):
        pltpu.make_async_copy(dst, dst, rsem).wait()

    sent = []
    xorder = [2, 1, 3, 0] if nx == 4 else list(range(1, nx)) + [0]
    order = [(dy, dx) for dy in (1, 0) for dx in xorder]
    loads = []
    for i, (dy, dx) in enumerate(order):
        c = hop(y, dy, ny) * nx + hop(x, dx, nx)
        at0 = c * blk
        if blk % 128 == 0:
            at0 = pl.multiple_of(at0, 128)
        cp = pltpu.make_async_copy(hid.at[:, :, pl.ds(at0, blk)], hv.at[i], hsem.at[i])
        cp.start()
        loads.append(cp)

    lane = lax.broadcasted_iota(jnp.int32, (1, 128), 1)
    row = lax.broadcasted_iota(jnp.int32, (2, 128), 0)
    lane2 = lax.broadcasted_iota(jnp.int32, (2, 128), 1)
    mine = jnp.where(row == 0, ids[0], ids[1])
    oh[g] = (mine == lane2).astype(F32)
    weights_old = jnp.ones((1, 128), F32)
    for k in range(old.shape[0]):
        weights_old = jnp.where(lane == k, old[k], weights_old)

    zero = jnp.zeros((ranks, toks), jnp.bfloat16)
    lhs = jnp.concatenate(
        [jnp.concatenate([lat[0], zero], axis=1), jnp.concatenate([zero, lat[1]], axis=1)], axis=0
    )

    def split(value):
        high = value.astype(BF16)
        return high, (value - high.astype(F32)).astype(BF16)

    def put(k, dst, terms):
        total = terms[0].astype(F32)
        for term in terms[1:]:
            total = total + term.astype(F32)
        if k == 0:
            dst(0)[...], dst(1)[...] = split(total)
        else:
            dst(1)[...] = (total + dst(1)[...].astype(F32)).astype(BF16)

    def first_sends(k, dy, dx, do_y=True, do_x=True):
        yy, xx = hop(y, dy, ny), hop(x, dx, nx)
        if dy and do_y:
            send(ys.at[k, yy, xx], yr.at[k, xx], ysend.at[k, dx], yrecv.at[k, dx], ypeer)
        if dx and do_x:
            send(
                xs.at[k, xx, yy], xr.at[k, dx - 1, yy], xsend.at[k, dx - 1, dy], xrecv.at[k, dx - 1, dy],
                xpeers[dx - 1],
            )

    def last_sends(k):
        for d in range(1, nz):
            send(zs.at[k, hop(z, d, nz)], zr.at[k, d - 1], zsend.at[k, d - 1], zrecv.at[k, d - 1], zpeers[d - 1])

    for i, (dy, dx) in enumerate(order):
        yy, xx = hop(y, dy, ny), hop(x, dx, nx)
        loads[i].wait()
        rhs = hv[i].reshape(2 * toks, blk)
        part = jnp.dot(lhs, rhs, preferred_element_type=F32)
        part = part.T.reshape(nz, RY + RX + RZ, cols)
        for k, half in enumerate(split(part)):
            ys[k, yy, xx] = half[:, :RY]
            xs[k, xx, yy] = half[:, RY : RY + RX]
            zs[k, :, yy, xx] = half[:, RY + RX :]
        if i == 0:
            pl.semaphore_wait(barrier, len(peers))
        first_sends(0, dy, dx)
    last_sends(0)
    for d, p in enumerate(lpeers):
        send(oh.at[g], oh.at[g], osend.at[d], orecv.at[d], p)
    last_sends(1)
    for dy, dx in order:
        first_sends(1, dy, dx, do_x=False)

    def first_y(k):
        for dx in xorder:
            xx = hop(x, dx, nx)
            wait(yr.at[k, xx], yrecv.at[k, dx])
            put(k, lambda j: y2s.at[j, xx], [ys[k, y, xx], yr[k, xx]])
            if dx:
                send(y2s.at[k, xx], y2r.at[k, dx - 1], y2send.at[k, dx - 1], y2recv.at[k, dx - 1], xpeers[dx - 1])

    def first_x(k):
        for dy in (1, 0):
            yy = hop(y, dy, ny)
            for d in range(1, nx):
                wait(xr.at[k, d - 1, yy], xrecv.at[k, d - 1, dy])
            put(k, lambda j: x2s.at[j, yy], [xs[k, x, yy]] + [xr[k, d - 1, yy] for d in range(1, nx)])
            if dy:
                send(x2s.at[k, yy], x2r.at[k], x2send.at[k], x2recv.at[k], ypeer)

    def first_z(k):
        for d in range(1, nz):
            wait(zr.at[k, d - 1], zrecv.at[k, d - 1])
        put(k, lambda j: z2s.at[j], [zs[k, z]] + [zr[k, d - 1] for d in range(1, nz)])
        send(z2s.at[k, 1 - y], z2r.at[k], z2send.at[k], z2recv.at[k], ypeer)

    def second_x(k):
        wait(x2r.at[k], x2recv.at[k])
        put(k, lambda j: x3s.at[j], [x2s[k, y], x2r[k]])
        for d in range(1, nz):
            send(x3s.at[k, hop(z, d, nz)], x3r.at[k, d - 1], x3send.at[k, d - 1], x3recv.at[k, d - 1], zpeers[d - 1])

    def second_y(k):
        for d in range(1, nx):
            wait(y2r.at[k, d - 1], y2recv.at[k, d - 1])
        put(k, lambda j: y3s.at[j], [y2s[k, x]] + [y2r[k, d - 1] for d in range(1, nx)])
        for d in range(1, nz):
            send(y3s.at[k, hop(z, d, nz)], y3r.at[k, d - 1], y3send.at[k, d - 1], y3recv.at[k, d - 1], zpeers[d - 1])

    def second_z(k):
        wait(z2r.at[k], z2recv.at[k])
        put(k, lambda j: z3s.at[j], [z2s[k, y], z2r[k]])
        for d in range(1, nx):
            send(z3s.at[k, hop(x, d, nx)], z3r.at[k, d - 1], z3send.at[k, d - 1], z3recv.at[k, d - 1], xpeers[d - 1])

    parts = ((0, RY), (RY, RX), (RY + RX, RZ))
    chips = nl // 2

    def third(k, own, r, rsem, n, part):
        lo, size = parts[part]
        for d in range(1, n):
            wait(r.at[k, d - 1], rsem.at[k, d - 1])
        put(k, lambda j: both.at[j, g, pl.ds(lo, size)], [own] + [r[k, d - 1] for d in range(1, n)])
        ref = both.at[k, g, pl.ds(lo, size)]
        for d, p in enumerate(lpeers):
            send(ref, ref, gsend.at[k, part, d], grecv.at[k, part, d], p)

    def third_x(k):
        third(k, x3s[k, z], x3r, x3recv, nz, 1)

    def third_z(k):
        third(k, z3s[k, x], z3r, z3recv, nx, 2)

    def third_y(k):
        third(k, y3s[k, z], y3r, y3recv, nz, 0)

    def low_x(k):
        for dy, dx in order:
            first_sends(1, dy, dx, do_y=False)

    def hand_over(k):
        for d in range(1, chips):
            src = hop(g, nl - 2 * d, nl)
            for part, (lo, size) in enumerate(parts):
                wait(both.at[k, src, pl.ds(lo, size)], grecv.at[k, part, d])
            send(both.at[k, src], both.at[k, src], fsend.at[k, d - 1], frecv.at[k, d - 1], lpeers[0])
            if k == 0:
                wait(oh.at[src], orecv.at[d])
                send(oh.at[src], oh.at[src], osend.at[chips + d - 1], orecv.at[chips + d - 1], lpeers[0])

    def take_over(k):
        for part, (lo, size) in enumerate(parts):
            wait(both.at[k, twin, pl.ds(lo, size)], grecv.at[k, part, 0])
        if k == 0:
            wait(oh.at[twin], orecv.at[0])
        for d in range(1, chips):
            src = hop(twin, nl - 2 * d, nl)
            wait(both.at[k, src], frecv.at[k, d - 1])
            if k == 0:
                wait(oh.at[src], orecv.at[chips + d - 1])

    steps = dict(
        y1=first_y, x1=first_x, z1=first_z, x2=second_x, y2=second_y, z2=second_z,
        x3=third_x, y3=third_y, z3=third_z, lx=low_x,
    )
    for step in ORDER:
        steps[step[:2]](int(step[2:] or 0))

    early = len(sent)
    hand_over(0)
    for step in LATE:
        steps[step[:2]](int(step[2:] or 0))
    take_over(0)

    slots = both[0].astype(F32)
    total = jnp.sum(slots, axis=0)
    twice = total + pltpu.roll(total, ranks, 1)
    prods = jnp.sum(slots * twice[None], axis=1)
    first_slot = lane < ranks
    dot0 = jnp.sum(jnp.where(first_slot, prods, 0.0), axis=1, keepdims=True)
    dot1 = jnp.sum(jnp.where(first_slot, 0.0, prods), axis=1, keepdims=True)
    square = jnp.sum(jnp.where(first_slot, jnp.sum(twice * twice, axis=0, keepdims=True), 0.0), axis=1, keepdims=True)
    oh0, oh1 = oh[:, 0, :], oh[:, 1, :]
    vec = jnp.sum(oh0 * dot0 + oh1 * dot1, axis=0, keepdims=True)
    langs = old.shape[0]
    vec = jnp.where(lane == langs, square, vec)

    ar[f] = vec
    n = ny * nx * nz

    def far(d):
        dy, dx, dz = d // (nx * nz), d // nz % nx, d % nz
        return dy + min(dx, nx - dx) + min(dz, nz - dz)

    for d in sorted(range(1, n), key=lambda d: -far(d)):
        yy, xx, zz = hop(y, d // (nx * nz), ny), hop(x, d // nz % nx, nx), hop(z, d % nz, nz)
        send(ar.at[f], ar.at[f], asend, arecv, at(yy, xx, zz), False)
    for c in sent[:early]:
        c.wait_send()
    hand_over(1)
    wait(ar.at[pl.ds(0, n - 1)], arecv)
    vec = jnp.sum(ar[...], axis=0)

    square = jnp.sum(jnp.where(lane == langs, vec, 0.0), axis=1, keepdims=True) + 1e-06
    valid = lane < langs
    logits = jnp.log(weights_old) + langs * (jnp.where(valid, vec, 0.0) / square)
    norm = jnp.log(jnp.sum(jnp.where(valid, jnp.exp(logits), 0.0), axis=1, keepdims=True))
    logw = logits - norm
    new_logw[...] = logw
    weights = jnp.where(valid, jnp.exp(logw), 0.0)
    w0 = jnp.sum(oh0 * weights, axis=1, keepdims=True)
    w1 = jnp.sum(oh1 * weights, axis=1, keepdims=True)
    slot_weight = jnp.where(first_slot, w0, w1)
    take_over(1)
    slots = slots + both[1].astype(F32)
    total = jnp.sum(slots * slot_weight[:, None, :], axis=0).T
    update[...] = total[:ranks] + total[ranks:]

    for c in sent[early:]:
        c.wait_send()
    pltpu.make_async_copy(ar.at[pl.ds(0, n - 1)], ar.at[pl.ds(0, n - 1)], asend).wait()


def adamw(grad, logw, param, first, second, new_param, new_first, new_second, new_logw):
    update = grad[...]
    m = 0.9 * first[...] + 0.1 * update
    v = 0.95 * second[...] + 0.05 * update * update
    new_first[...] = m
    new_second[...] = v
    m_hat = m / (1.0 - 0.9**STEP)
    v_hat = v / (1.0 - 0.95**STEP)
    p = param[...]
    new_param[...] = p - 0.02 * (m_hat / (jnp.sqrt(v_hat) + 1e-08) + 0.1 * p)
    new_logw[...] = logw[0, : new_logw.shape[0]]


def local(nl, ny, nx, nz, hidden, latent_grad, lang_ids, old_weights, param, first_moment, second_moment):
    rows, ranks = param.shape
    cols = 2 * ranks
    assert rows == RY + RX + RZ and hidden.shape[0] == 2
    blk = hidden.shape[2] // (ny * nx)
    vmem = pl.BlockSpec(memory_space=pltpu.VMEM)
    smem = pl.BlockSpec(memory_space=pltpu.SMEM)
    dma = pltpu.SemaphoreType.DMA
    b = lambda *s: pltpu.VMEM((2,) + s + (cols,), BF16)
    dma2 = lambda *s: dma((2,) + s)
    mat = jax.ShapeDtypeStruct((ranks, rows), F32)
    scratch = [
        pltpu.VMEM((ny * nx, 2, hidden.shape[1], blk), jnp.bfloat16),
        b(ny, nx, nz, RY), b(nx, ny, nz, RX), b(nz, ny, nx, RZ),
        b(nx, nz, RY), b(nx - 1, ny, nz, RX), b(nz - 1, ny, nx, RZ),
        b(nx, nz, RY), b(ny, nz, RX), b(ny, nx, RZ),
        b(nx - 1, nz, RY), b(nz, RX), b(nx, RZ),
        b(nz, RY), b(nz, RX), b(nx, RZ),
        b(nz - 1, RY), b(nz - 1, RX), b(nx - 1, RZ),
        b(nl, rows),
        pltpu.VMEM((nl, 2, 128), F32),
        pltpu.VMEM((ny * nx * nz, 1, 128), F32),
        dma((ny * nx,)),
        dma2(nx), dma2(nx), dma2(nx - 1, ny), dma2(nx - 1, ny), dma2(nz - 1), dma2(nz - 1),
        dma2(nx - 1), dma2(nx - 1), dma2(), dma2(), dma2(), dma2(),
        dma2(nz - 1), dma2(nz - 1), dma2(nz - 1), dma2(nz - 1), dma2(nx - 1), dma2(nx - 1),
        dma2(3, nl // 2), dma2(3, nl // 2), dma2(max(nl // 2 - 1, 1)), dma2(max(nl // 2 - 1, 1)), dma((nl - 1,)), dma((nl - 1,)),
        dma, dma,
    ]
    update, logw = pl.pallas_call(
        functools.partial(kernel, nl, ny, nx, nz),
        out_shape=(mat, jax.ShapeDtypeStruct((1, 128), F32)),
        in_specs=[pl.BlockSpec(memory_space=pl.ANY), vmem, smem, smem],
        out_specs=(vmem, vmem),
        scratch_shapes=scratch,
        compiler_params=pltpu.CompilerParams(
            collective_id=0, has_side_effects=True, vmem_limit_bytes=61 * 1024 * 1024
        ),
        name="reweight",
    )(hidden, latent_grad.transpose(0, 2, 1), lang_ids, old_weights)
    outs = pl.pallas_call(
        adamw,
        out_shape=(mat, mat, mat, jax.ShapeDtypeStruct(old_weights.shape, F32)),
        in_specs=[vmem] * 5,
        out_specs=(vmem,) * 4,
        name="adamw",
    )(update, logw, param.T, first_moment.T, second_moment.T)
    return (outs[0].T, outs[1].T, outs[2].T, outs[3])


def solution(mesh):
    nl = mesh.shape["language"]
    ny, nx, nz = GRID[mesh.shape["fsdp"]]
    placed = (
        P("language", "fsdp", None),
        P("language", "fsdp", None),
        P("language"),
        P(),
        P("fsdp", None),
        P("fsdp", None),
        P("fsdp", None),
    )
    return jax.shard_map(
        functools.partial(local, nl, ny, nx, nz),
        mesh=mesh,
        in_specs=placed,
        out_specs=(P("fsdp", None), P("fsdp", None), P("fsdp", None), P()),
        check_vma=False,
    )
```
